32 devices in a mesh: row: 8 (over y, x, core), col: 4 (over z).
Axes of the slice: x: 2, y: 2, z: 4, core: 2. Of those that a mesh axis runs over, the one named last changes fastest.
Arguments:
- object_slices: float32 [2, 2, 1024, 512], P(None, None, 'row', 'col'), may hold values from -4 to 4
- probe_wave: bfloat16 [2, 256, 256], replicated, may hold values from -4 to 4
- propagator_phase: bfloat16 [256, 256], replicated, may hold values from -3.140625 to 3.140625
- intensity: bfloat16 [8, 4, 2, 256, 256], P('row', 'col'), may hold values from 0.099609375 to 3
- centres: int32 [8, 4, 2, 2], P('row', 'col'), may hold values from 0 to 1023, as said below
- batch_order: int32 [8, 4, 2], P('row', 'col'), may hold values from -1 to 30, as said below
Outputs:
- object_gradient: float32 [2, 2, 1024, 512], P(None, None, 'row', 'col')
- probe_gradient: float32 [2, 256, 256], P(None, 'row', 'col')
The draws below stay inside these ranges and needn't reach their ends.
Inputs may be any that keep to these rules, and one draw needn't show every extreme that they name: `centres`: slot c of tile (g, h) holds (row, column) pixel coordinates in the whole object that lie in that tile: rows g * 128 to (g + 1) * 128 - 1, columns h * 128 to (h + 1) * 128 - 1; empty slots hold a point of their tile too. `batch_order`: -1 marks an empty slot; the live slots of a tile come first and are numbered 0, 1, 2, ... in batch order, tile after tile in row-major order of tiles; some tile has all 2 slots live and some tile has none.
All inputs are finite; a program needn't handle non-finite values.
Results may differ from the reference program's by a relative error of at most 0.0003.
Values sent between devices are 32-bit elements; how exact they have to be, the bound alone decides.
A program may use at most 64 MiB of HBM per device.

```python
import math
import jax
import jax.numpy as jnp
from jax import lax

WIN = 256
SLICES = 2
TILE_R = 128
TILE_C = 128
SLOTS = 2
GRID_R = 8
GRID_C = 4
OBJ_R = 1024
OBJ_C = 512


def draw_centres(key, part):
    key = jax.random.fold_in(key, 23)
    row_key, col_key = jax.random.split(key)
    tile_top = (jnp.arange(GRID_R, dtype=jnp.int32) * TILE_R)[:, None, None]
    tile_left = (jnp.arange(GRID_C, dtype=jnp.int32) * TILE_C)[None, :, None]
    row_values = jax.random.randint(row_key, (GRID_R, GRID_C, SLOTS), 0, TILE_R) + tile_top
    col_values = jax.random.randint(col_key, (GRID_R, GRID_C, SLOTS), 0, TILE_C) + tile_left
    row_values = row_values.at[0, 0, 0].set(0).at[GRID_R - 1, GRID_C - 1, 0].set(OBJ_R - 1)
    col_values = col_values.at[0, 0, 0].set(0).at[GRID_R - 1, GRID_C - 1, 0].set(OBJ_C - 1)
    return jnp.stack([row_values, col_values], axis=-1).astype(jnp.int32)


def draw_batch_order(key, part):
    key = jax.random.fold_in(key, 41)
    tiles = GRID_R * GRID_C
    base_counts = jnp.arange(tiles, dtype=jnp.int32) % (SLOTS + 1)
    counts = jax.random.permutation(key, base_counts)
    slot_index = jnp.arange(SLOTS, dtype=jnp.int32)
    filled = (slot_index[None, :] < counts[:, None]).reshape(-1).astype(jnp.int32)
    ranked = jnp.cumsum(filled) - 1
    ordered = jnp.where(filled > 0, ranked, -1)
    return ordered.reshape(GRID_R, GRID_C, SLOTS).astype(jnp.int32)


def levels(key, shape, cuts, least, high):
    gain = 1.0
    for axis_at, blocks in cuts:
        steps = jax.random.uniform(jax.random.fold_in(jax.random.fold_in(key, 6), axis_at), (blocks,), jnp.float32, least / len(cuts), high / len(cuts))
        gain = gain * jnp.repeat(jnp.exp(steps), shape[axis_at] // blocks).reshape((-1,) + (1,) * (len(shape) - 1 - axis_at))
    return gain


def bell_draw(own_key, extent, spread, most, cuts=(), kind=jnp.bfloat16):
    values = jax.random.normal(own_key, extent, jnp.float32) * spread
    if len(cuts) > 0:
        values = levels(own_key, extent, cuts, -0.22, 0.18) * values
    return jnp.clip(values, min=-most, max=most).astype(kind)


def setup_inputs(seed: int = 0) -> dict:
    arg_keys = jax.random.split(jax.random.key(seed), 7)
    object_slices = bell_draw(arg_keys[0], (SLICES, 2, OBJ_R, OBJ_C), 0.7, 4.0, ((2, 8), (3, 4)), jnp.float32)
    probe_wave = bell_draw(arg_keys[1], (2, WIN, WIN), 0.7, 4.0)
    propagator_phase = jnp.clip(jax.random.uniform(arg_keys[2], (WIN, WIN), jnp.float32, -3.140625, 3.140625), -3.140625, 3.140625).astype(jnp.bfloat16)
    intensity = jnp.clip(jnp.exp(math.log(3.0) - 3.4051113 * jax.random.uniform(arg_keys[3], (GRID_R, GRID_C, SLOTS, WIN, WIN), jnp.float32) ** levels(arg_keys[3], (GRID_R, GRID_C, SLOTS, WIN, WIN), ((0, 8), (1, 4)), -0.2, 0.2)), 0.099609375, 3.0).astype(jnp.bfloat16)
    centres = draw_centres(jax.random.fold_in(arg_keys[6], 71), 0)
    batch_order = draw_batch_order(jax.random.fold_in(arg_keys[6], 71), 0)
    return dict(object_slices=object_slices, probe_wave=probe_wave, propagator_phase=propagator_phase, intensity=intensity, centres=centres, batch_order=batch_order)


def complex_pair(values):
    return jnp.stack([jnp.real(values), jnp.imag(values)])


def position_terms(padded, probe_field, propagator, row_start, col_start, measured, weight):
    zero_index = jnp.zeros((), jnp.int32)
    anchor = (zero_index, zero_index, row_start.astype(jnp.int32), col_start.astype(jnp.int32))
    window = lax.dynamic_slice(padded, anchor, (SLICES, 2, WIN, WIN))
    layers = lax.complex(window[:, 0], window[:, 1])
    wave_field = probe_field
    entering = []
    for slice_index in range(SLICES):
        entering.append(wave_field)
        spectrum = jnp.fft.fft2(wave_field * layers[slice_index], norm="ortho")
        if slice_index + 1 < SLICES:
            wave_field = jnp.fft.ifft2(spectrum * propagator, norm="ortho")
    power_map = jnp.real(spectrum) ** 2 + jnp.imag(spectrum) ** 2
    misfit = weight * (power_map - measured)
    adjoint = jnp.fft.ifft2(misfit * spectrum, norm="ortho")
    object_terms = [None] * SLICES
    for slice_index in reversed(range(SLICES)):
        object_terms[slice_index] = complex_pair(jnp.conj(entering[slice_index]) * adjoint)
        upstream = jnp.conj(layers[slice_index]) * adjoint
        if slice_index > 0:
            adjoint = jnp.fft.ifft2(jnp.fft.fft2(upstream, norm="ortho") * jnp.conj(propagator), norm="ortho")
    return jnp.stack(object_terms), complex_pair(upstream)


def reference(object_slices, probe_wave, propagator_phase, intensity, centres, batch_order):
    half_win = WIN // 2
    padded = jnp.pad(object_slices, ((0, 0), (0, 0), (half_win, half_win), (half_win, half_win)))
    probe_field = lax.complex(probe_wave[0].astype(jnp.float32), probe_wave[1].astype(jnp.float32))
    angles = propagator_phase.astype(jnp.float32)
    propagator = lax.complex(jnp.cos(angles), jnp.sin(angles))
    centre_list = centres.reshape(-1, 2).astype(jnp.int32)
    weights = (batch_order.reshape(-1) >= 0).astype(jnp.float32)
    measured = intensity.reshape(-1, WIN, WIN)

    def advance(state_pair, inputs):
        gradient, probe_sum = state_pair
        centre_pair, weight, frame_data = inputs
        window_terms, upstream = position_terms(padded, probe_field, propagator, centre_pair[0], centre_pair[1], frame_data.astype(jnp.float32), weight)
        zero_index = jnp.zeros((), jnp.int32)
        anchor = (zero_index, zero_index, centre_pair[0].astype(jnp.int32), centre_pair[1].astype(jnp.int32))
        current = lax.dynamic_slice(gradient, anchor, window_terms.shape)
        gradient = lax.dynamic_update_slice(gradient, current + window_terms, anchor)
        return (gradient, probe_sum + upstream), None

    initial = (jnp.zeros(padded.shape, jnp.float32), jnp.zeros((2, WIN, WIN), jnp.float32))
    (gradient, probe_sum), unused = lax.scan(advance, initial, (centre_list, weights, measured))
    return gradient[:, :, half_win:half_win + OBJ_R, half_win:half_win + OBJ_C], probe_sum
```

```python
import functools
import math

import jax
import jax.numpy as jnp
import ml_dtypes
import numpy as np
from jax import lax
from jax.experimental import pallas as pl
from jax.experimental.pallas import tpu as pltpu
from jax.sharding import PartitionSpec as P


def shift_pair(value, axis, dim, width):
    devices, length = (lax.axis_size(axis), value.shape[dim])
    up = [(i, (i + 1) % devices) for i in range(devices - 1)]
    down = [(j, i) for i, j in up]
    last = lax.slice_in_dim(value, length - width, length, axis=dim)
    leading = lax.slice_in_dim(value, 0, width, axis=dim)
    return lax.ppermute(last, axis, up), lax.ppermute(leading, axis, down)


def with_halo(value, sides, width):
    for axis, dim in sides:
        before, after = shift_pair(value, axis, dim, width)
        value = jnp.concatenate([before, value, after], axis=dim)
    return value


def fold(value, sides, width):
    for axis, dim in sides:
        before, after = shift_pair(value, axis, dim, width)
        length = value.shape[dim] - 2 * width
        middle = lax.slice_in_dim(value, width, width + length, axis=dim)
        if length == width:
            value = middle + before + after
        else:
            pads = [(0, 0)] * value.ndim
            pads[dim] = (0, length - width)
            first = jnp.pad(before, pads)
            pads[dim] = (length - width, 0)
            value = middle + first + jnp.pad(after, pads)
    return value


def halve(value, axis, dim):
    devices = lax.axis_size(axis)
    index = lax.axis_index(axis)
    bits = devices.bit_length() - 1
    shape = value.shape
    value = value.reshape(shape[:dim] + (2,) * bits + (shape[dim] // devices,) + shape[dim + 1 :])
    for bit in range(bits):
        at = dim + bits - 1 - bit
        mine = lax.rem(index // (1 << bit), 2)
        kept = lax.dynamic_index_in_dim(value, mine, at, keepdims=False)
        sent = lax.dynamic_index_in_dim(value, 1 - mine, at, keepdims=False)
        pairs = [(i, i ^ (1 << bit)) for i in range(devices)]
        value = kept + lax.ppermute(sent, axis, pairs)
    return value


def split(value):
    high = value.astype(jnp.bfloat16)
    low = (value - high.astype(jnp.float32)).astype(jnp.bfloat16)
    return high, low


def tables(width):
    index = np.arange(width)
    angles = (np.outer(index, index) % width) * (2.0 * math.pi / width)
    cosine = np.cos(angles) / math.sqrt(width)
    sine = np.sin(angles) / math.sqrt(width)
    out = []
    for orient in (-1.0, 1.0):
        block = np.block([[cosine, orient * sine], [-orient * sine, cosine]]).astype(np.float32)
        high = block.astype(ml_dtypes.bfloat16)
        low = (block - high.astype(np.float32)).astype(ml_dtypes.bfloat16)
        out += [high, low]
    return out


def dot(left, right):
    return jnp.dot(left, right, preferred_element_type=jnp.float32)


def make_transform(forward, inverse, width):
    def transform(values, orient):
        first, second = (forward, inverse) if orient < 0 else (inverse, forward)
        high, low = split(jnp.concatenate(values, axis=1))
        table = first[0][...]
        once = dot(high, table) + dot(low, table) + dot(high, first[1][...])
        high, low = split(jnp.concatenate([once[:, :width], once[:, width:]], axis=0))
        table = second[0][...]
        twice = dot(table, high) + dot(table, low) + dot(second[1][...], high)
        return (twice[:width], twice[width:])

    return transform


def product(left, right):
    return (left[0] * right[0] - left[1] * right[1], left[0] * right[1] + left[1] * right[0])


def conjugate(values):
    return (values[0], -values[1])


def kernel(starts, live, ext, probe, prop, intensity, fh, fl, ih, il, grad, pgrad, padded):
    slices = ext.shape[0]
    width = probe.shape[1]
    rows, cols = ext.shape[2], ext.shape[3]
    slot_count = intensity.shape[0]
    transform = make_transform((fh, fl), (ih, il), width)
    grad[...] = jnp.zeros_like(grad)
    pgrad[...] = jnp.zeros_like(pgrad)
    padded[...] = jnp.zeros_like(padded)

    def slot_body(slot, carry):
        row = starts[slot, 0]
        col = starts[slot, 1]

        def window(s):
            parts = []
            for c in range(2):
                band = pltpu.roll(ext[s, c], lax.rem(rows - row, rows), 0)[:width]
                parts.append(pltpu.roll(band, lax.rem(cols - col, cols), 1)[:, :width])
            return tuple(parts)

        def place(s, values):
            for c in range(2):
                padded[:width, :width] = values[c]
                band = pltpu.roll(padded[...], row, 0)
                grad[s, c] += pltpu.roll(band, col, 1)

        field = (probe[0].astype(jnp.float32), probe[1].astype(jnp.float32))
        propagator = (prop[0], prop[1])
        layers, entering = [], []
        for s in range(slices):
            entering.append(field)
            layers.append(window(s))
            spectrum = transform(product(field, layers[s]), -1.0)
            if s + 1 < slices:
                field = transform(product(spectrum, propagator), 1.0)
        measured = intensity[slot].astype(jnp.float32)
        weight = jnp.where(live[slot] >= 0, 1.0, 0.0).astype(jnp.float32)
        misfit = weight * (spectrum[0] * spectrum[0] + spectrum[1] * spectrum[1] - measured)
        adjoint = transform((misfit * spectrum[0], misfit * spectrum[1]), 1.0)
        for s in reversed(range(slices)):
            place(s, product(conjugate(entering[s]), adjoint))
            upstream = product(conjugate(layers[s]), adjoint)
            if s > 0:
                adjoint = transform(
                    product(transform(upstream, -1.0), conjugate(propagator)), 1.0
                )
        pgrad[0] += upstream[0]
        pgrad[1] += upstream[1]
        return carry

    lax.fori_loop(0, slot_count, slot_body, 0)


def gradients(starts, live, extended, probe, prop, intensity):
    width = probe.shape[1]
    rows, cols = extended.shape[2:]
    smem = pl.BlockSpec(memory_space=pltpu.SMEM)
    vmem = pl.BlockSpec(memory_space=pltpu.VMEM)
    flops = intensity.shape[0] * 6 * 2 * 3 * 2 * width * 4 * width * width
    return pl.pallas_call(
        kernel,
        out_shape=(
            jax.ShapeDtypeStruct(extended.shape, jnp.float32),
            jax.ShapeDtypeStruct((2, width, width), jnp.float32),
        ),
        in_specs=[smem] * 2 + [vmem] * 8,
        out_specs=(vmem, vmem),
        scratch_shapes=[pltpu.VMEM((rows, cols), jnp.float32)],
        compiler_params=pltpu.CompilerParams(vmem_limit_bytes=48 * 2**20),
        cost_estimate=pl.CostEstimate(flops=flops, bytes_accessed=10 * 2**20, transcendentals=0),
    )(starts, live, extended, probe, prop, intensity, *tables(width))


def per_device(object_slices, probe_wave, propagator_phase, intensity, centres, batch_order):
    tile_rows, tile_cols = object_slices.shape[2:]
    width = probe_wave.shape[1]
    half_win = width // 2
    extended = with_halo(object_slices, (("row", 2), ("col", 3)), half_win)
    origin = jnp.stack([lax.axis_index("row") * tile_rows, lax.axis_index("col") * tile_cols])
    starts = (centres[0, 0] - origin[None]).astype(jnp.int32)
    angles = propagator_phase.astype(jnp.float32)
    prop = jnp.stack([jnp.cos(angles), jnp.sin(angles)])
    accumulated, probe_term = gradients(
        starts, batch_order[0, 0], extended, probe_wave, prop, intensity[0, 0]
    )
    object_gradient = fold(accumulated, (("col", 3), ("row", 2)), half_win)
    probe_gradient = halve(halve(probe_term, "row", 1), "col", 2)
    return (object_gradient, probe_gradient)


def solution(mesh):
    placed = (
        P(None, None, "row", "col"),
        P(),
        P(),
        P("row", "col", None, None, None),
        P("row", "col", None, None),
        P("row", "col", None),
    )
    return jax.shard_map(
        per_device,
        mesh=mesh,
        in_specs=placed,
        out_specs=(P(None, None, "row", "col"), P(None, "row", "col")),
        check_vma=False,
    )
```

```python
import math

import jax
import jax.numpy as jnp
import ml_dtypes
import numpy as np
from jax import lax
from jax.experimental import pallas as pl
from jax.experimental.pallas import tpu as pltpu
from jax.sharding import PartitionSpec as P

MESH = pl.DeviceIdType.MESH


def split(value):
    high = value.astype(jnp.bfloat16)
    low = (value - high.astype(jnp.float32)).astype(jnp.bfloat16)
    return high, low


def tables(width):
    index = np.arange(width)
    angles = (np.outer(index, index) % width) * (2.0 * math.pi / width)
    cosine = np.cos(angles) / math.sqrt(width)
    sine = np.sin(angles) / math.sqrt(width)
    out = []
    for orient in (-1.0, 1.0):
        block = np.block([[cosine, orient * sine], [-orient * sine, cosine]]).astype(np.float32)
        high = block.astype(ml_dtypes.bfloat16)
        low = (block - high.astype(np.float32)).astype(ml_dtypes.bfloat16)
        out += [high, low]
    return out


def dot(left, right):
    return jnp.dot(left, right, preferred_element_type=jnp.float32)


def make_transform(forward, inverse, width):
    def transform(values, orient):
        first, second = (forward, inverse) if orient < 0 else (inverse, forward)
        high, low = split(jnp.concatenate(values, axis=1))
        table = first[0][...]
        once = dot(high, table) + dot(low, table) + dot(high, first[1][...])
        high, low = split(jnp.concatenate([once[:, :width], once[:, width:]], axis=0))
        table = second[0][...]
        twice = dot(table, high) + dot(table, low) + dot(second[1][...], high)
        return (twice[:width], twice[width:])

    return transform


def product(left, right):
    return (left[0] * right[0] - left[1] * right[1], left[0] * right[1] + left[1] * right[0])


def conjugate(values):
    return (values[0], -values[1])


def kernel(
    centres, live, tile, probe, phase, intensity, tables_hbm, out, probe_out,
    table, ext, acc, field_one, upstream_one, adjoint_zero, prop,
    first_cols, first_rows, last_in, mid_cols, mid_rows,
    terms, arrived, blocks, blocks_in, table_sem,
    halo_send, halo_recv, fold_send, fold_recv, sum_send, sum_recv,
):
    slices, slot_count = tile.shape[0], intensity.shape[0]
    width = probe.shape[1]
    half = width // 2
    size = tile.shape[2] + width
    sizes = {"row": lax.axis_size("row"), "col": lax.axis_size("col")}
    at = {"row": lax.axis_index("row"), "col": lax.axis_index("col")}
    bits = {name: sizes[name].bit_length() - 1 for name in sizes}
    steps = [("row", bit) for bit in range(bits["row"])] + [("col", bit) for bit in range(bits["col"])]
    first, middle, last = pl.ds(0, half), pl.ds(half, half), pl.ds(2 * half, half)
    every = pl.ds(0, size)

    def has(axis, delta):
        return at[axis] > 0 if delta < 0 else at[axis] < sizes[axis] - 1

    def partner(axis, bit):
        odd = lax.rem(at[axis] // (1 << bit), 2)
        return odd, at[axis] + (1 - 2 * odd) * (1 << bit)

    barrier = pltpu.get_barrier_semaphore()
    count = 0
    for axis in ("row", "col"):
        for delta in (-1, 1):
            @pl.when(has(axis, delta))
            def _(axis=axis, delta=delta):
                pl.semaphore_signal(barrier, inc=1, device_id={axis: at[axis] + delta}, device_id_type=MESH)
            count = count + jnp.where(has(axis, delta), 1, 0)
    for axis, bit in steps:
        if bit > 0:
            pl.semaphore_signal(barrier, inc=1, device_id={axis: partner(axis, bit)[1]}, device_id_type=MESH)
            count = count + 1
    pl.semaphore_wait(barrier, count)

    class Shift:
        def __init__(self, src, dst, send, recv, axis, delta):
            n = sizes[axis]
            self.copy = pltpu.make_async_remote_copy(
                src_ref=src, dst_ref=dst, send_sem=send, recv_sem=recv,
                device_id={axis: lax.rem(at[axis] + delta + n, n)}, device_id_type=MESH,
            )
            self.target, self.source = has(axis, delta), has(axis, -delta)

        def start(self):
            pl.when(self.target)(lambda: self.copy.start())

        def wait_recv(self):
            pl.when(self.source)(lambda: self.copy.wait_recv())

        def wait_send(self):
            pl.when(self.target)(lambda: self.copy.wait_send())

    def halo(s, part):
        copies = []
        for side, delta in enumerate((1, -1)):
            place = first if delta > 0 else last
            for c in range(2):
                if c == 0 and part == 0:
                    src, dst, axis = tile.at[s, c], ext[s][c].at[place, middle], "row"
                elif c == 0:
                    src, dst, axis = ext[s][c].at[every, middle], ext[s][c].at[every, place], "col"
                elif part == 0:
                    src, dst, axis = tile.at[s, c], ext[s][c].at[middle, place], "col"
                else:
                    src, dst, axis = ext[s][c].at[middle, every], ext[s][c].at[place, every], "row"
                sem = ((s * 2 + part) * 2 + c) * 2 + side
                copies.append(Shift(src, dst, halo_send.at[sem], halo_recv.at[sem], axis, delta))
        return copies

    def folding(s, part):
        copies = []
        for side, delta in enumerate((1, -1)):
            place = last if delta > 0 else first
            for c in range(2):
                if c == 0 and part == 0:
                    src, dst, axis = acc[s][c].at[every, place], first_cols[s][side], "col"
                elif c == 0:
                    src, dst, axis = mid_cols[s].at[place, :], last_in[s][c][side], "row"
                elif part == 0:
                    src, dst, axis = acc[s][c].at[place, every], first_rows[s][side], "row"
                else:
                    src, dst, axis = mid_rows[s].at[:, place], last_in[s][c][side], "col"
                sem = ((s * 2 + part) * 2 + c) * 2 + side
                copies.append(Shift(src, dst, fold_send.at[sem], fold_recv.at[sem], axis, delta))
        return copies

    def start_all(copies):
        for copy in copies:
            copy.start()
        sent.extend(copies)

    def arrive_all(copies):
        for copy in copies:
            copy.wait_recv()

    sent = []
    halos = [[halo(s, part) for part in range(2)] for s in range(slices)]
    folds = [[folding(s, part) for part in range(2)] for s in range(slices)]
    for s in range(slices):
        start_all(halos[s][0])
    loads = [pltpu.make_async_copy(tables_hbm.at[k], table.at[k], table_sem.at[k]) for k in range(4)]
    for load in loads:
        load.start()

    for s in range(slices):
        for c in range(2):
            ext[s][c][middle, middle] = tile[s, c]
        for side, delta in enumerate((1, -1)):
            place = first if delta > 0 else last

            @pl.when(jnp.logical_not(has("row", -delta)))
            def _(s=s, side=side, place=place):
                ext[s][0][place, middle] = jnp.zeros((half, half), jnp.float32)
                ext[s][1][place, every] = jnp.zeros((half, size), jnp.float32)
                first_rows[s][side][...] = jnp.zeros((half, size), jnp.float32)
                last_in[s][0][side][...] = jnp.zeros((half, half), jnp.float32)

            @pl.when(jnp.logical_not(has("col", -delta)))
            def _(s=s, side=side, place=place):
                ext[s][1][middle, place] = jnp.zeros((half, half), jnp.float32)
                ext[s][0][every, place] = jnp.zeros((size, half), jnp.float32)
                first_cols[s][side][...] = jnp.zeros((size, half), jnp.float32)
                last_in[s][1][side][...] = jnp.zeros((half, half), jnp.float32)

    for s in range(slices):
        arrive_all(halos[s][0])
        start_all(halos[s][1])

    angles = phase[...].astype(jnp.float32)
    prop[0] = jnp.cos(angles)
    prop[1] = jnp.sin(angles)
    for load in loads:
        load.wait()
    arrive_all(halos[0][1])

    transform = make_transform(
        (table.at[0], table.at[1]), (table.at[2], table.at[3]), width
    )

    def start_of(slot):
        row = centres[slot, 0] - at["row"] * tile.shape[2]
        return row, centres[slot, 1] - at["col"] * tile.shape[3]

    def window(s, slot):
        row, col = start_of(slot)
        parts = []
        for c in range(2):
            band = pltpu.roll(ext[s][c][...], lax.rem(size - row, size), 0)[:width]
            parts.append(pltpu.roll(band, lax.rem(size - col, size), 1)[:, :width])
        return tuple(parts)

    def place_term(s, slot, values):
        row, col = start_of(slot)
        for c in range(2):
            wide = jnp.concatenate([values[c], jnp.zeros((width, size - width), jnp.float32)], axis=1)
            wide = pltpu.roll(wide, col, 1)
            tall = jnp.concatenate([wide, jnp.zeros((size - width, size), jnp.float32)], axis=0)
            acc[s][c][...] += pltpu.roll(tall, row, 0)

    def entering_zero():
        return (probe[0].astype(jnp.float32), probe[1].astype(jnp.float32))

    def pair(ref, slot):
        return (ref[slot, 0], ref[slot, 1])

    def keep(ref, slot, values):
        ref[slot, 0] = values[0]
        ref[slot, 1] = values[1]

    for s in range(slices):
        for c in range(2):
            acc[s][c][...] = jnp.zeros((size, size), jnp.float32)
    terms[0][...] = jnp.zeros(terms[0].shape, jnp.float32)

    def forward(slot, carry):
        spectrum = transform(product(entering_zero(), window(0, slot)), -1.0)
        keep(field_one, slot, transform(product(spectrum, (prop[0], prop[1])), 1.0))
        return carry

    lax.fori_loop(0, slot_count, forward, 0)
    arrive_all(halos[1][1])

    def turn(slot, carry):
        layer = window(1, slot)
        field = pair(field_one, slot)
        spectrum = transform(product(field, layer), -1.0)
        measured = intensity[slot].astype(jnp.float32)
        weight = jnp.where(live[slot] >= 0, 1.0, 0.0).astype(jnp.float32)
        misfit = weight * (spectrum[0] * spectrum[0] + spectrum[1] * spectrum[1] - measured)
        adjoint = transform((misfit * spectrum[0], misfit * spectrum[1]), 1.0)
        place_term(1, slot, product(conjugate(field), adjoint))
        keep(upstream_one, slot, product(conjugate(layer), adjoint))
        return carry

    lax.fori_loop(0, slot_count, turn, 0)
    start_all(folds[1][0])

    def fold_middle(s):
        arrive_all(folds[s][0])
        mid_cols[s][...] = acc[s][0][every, middle] + first_cols[s][0][...] + first_cols[s][1][...]
        mid_rows[s][...] = acc[s][1][middle, every] + first_rows[s][0][...] + first_rows[s][1][...]
        start_all(folds[s][1])

    def fold_end(s):
        arrive_all(folds[s][1])
        out[s, 0] = mid_cols[s][middle, :] + last_in[s][0][0][...] + last_in[s][0][1][...]
        out[s, 1] = mid_rows[s][:, middle] + last_in[s][1][0][...] + last_in[s][1][1][...]

    def back(slot, carry):
        spectrum = transform(pair(upstream_one, slot), -1.0)
        adjoint = transform(product(spectrum, conjugate((prop[0], prop[1]))), 1.0)
        keep(adjoint_zero, slot, adjoint)
        upstream = product(conjugate(window(0, slot)), adjoint)
        for c in range(2):
            terms[0][c] += upstream[c].reshape(terms[0].shape[1:])
        pl.when(slot == 0)(lambda: fold_middle(1))
        return carry

    lax.fori_loop(0, slot_count, back, 0)

    def halving(step):
        axis, bit = steps[step]
        odd, other = partner(axis, bit)
        held = terms[step] if axis == "row" else blocks[bit]
        landing = arrived[step] if axis == "row" else blocks_in[bit]
        copy = pltpu.make_async_remote_copy(
            src_ref=held.at[:, :, 1 - odd], dst_ref=landing,
            send_sem=sum_send.at[step], recv_sem=sum_recv.at[step],
            device_id={axis: other}, device_id_type=MESH,
        )
        return copy, held, landing, odd

    halvings = [halving(step) for step in range(len(steps))]

    def sum_next(step):
        copy, held, landing, odd = halvings[step]
        copy.wait()
        total = held[:, :, odd] + landing[...]
        if step + 1 == len(steps):
            probe_out[...] = total[:, 0, :, : probe_out.shape[2]]
            return
        if step + 1 < bits["row"]:
            terms[step + 1][...] = total.reshape(terms[step + 1].shape)
        elif step + 1 == bits["row"]:
            span = probe_out.shape[2]
            for j in range(sizes["col"]):
                blocks[0][:, j // 2, j % 2, :, :span] = total[:, 0, :, j * span : (j + 1) * span]
        else:
            following = blocks[step + 1 - bits["row"]]
            following[...] = total.reshape(following.shape)
        halvings[step + 1][0].start()

    if blocks[0].shape[-1] > probe_out.shape[2]:
        blocks[0][...] = jnp.zeros(blocks[0].shape, jnp.float32)
    halvings[0][0].start()

    def place_zero(slot, carry):
        place_term(0, slot, product(conjugate(entering_zero()), pair(adjoint_zero, slot)))
        return carry

    lax.fori_loop(0, slot_count, place_zero, 0)
    start_all(folds[0][0])
    sum_next(0)
    fold_end(1)
    sum_next(1)
    fold_middle(0)
    for step in range(2, len(steps) - 1):
        sum_next(step)
    fold_end(0)
    sum_next(len(steps) - 1)
    for copy in sent:
        copy.wait_send()


def per_device(object_slices, probe_wave, propagator_phase, intensity, centres, batch_order):
    slices = object_slices.shape[0]
    half = object_slices.shape[2]
    width = probe_wave.shape[1]
    size = half + width
    slot_count = centres.shape[2]
    rows, cols = lax.axis_size("row"), lax.axis_size("col")
    block_rows, block_cols = width // rows, width // cols
    lanes = max(block_cols, 128)
    row_bits, col_bits = rows.bit_length() - 1, cols.bit_length() - 1
    smem = pl.BlockSpec(memory_space=pltpu.SMEM)
    vmem = pl.BlockSpec(memory_space=pltpu.VMEM)

    def floats(*shape):
        return pltpu.VMEM(shape, jnp.float32)

    def sems(count):
        return pltpu.SemaphoreType.DMA((count,))

    slot_fields = floats(slot_count, 2, width, width)
    scratch = [
        pltpu.VMEM((4, 2 * width, 2 * width), jnp.bfloat16),
        [[floats(size, size)] * 2] * slices,
        [[floats(size, size)] * 2] * slices,
        slot_fields,
        slot_fields,
        slot_fields,
        floats(2, width, width),
        [[floats(size, half)] * 2] * slices,
        [[floats(half, size)] * 2] * slices,
        [[[floats(half, half)] * 2] * 2] * slices,
        [floats(size, half)] * slices,
        [floats(half, size)] * slices,
        [floats(2, rows >> (k + 1), 2, block_rows, width) for k in range(row_bits)],
        [floats(2, rows >> (k + 1), block_rows, width) for k in range(row_bits)],
        [floats(2, cols >> (k + 1), 2, block_rows, lanes) for k in range(col_bits)],
        [floats(2, cols >> (k + 1), block_rows, lanes) for k in range(col_bits)],
        sems(4),
        sems(8 * slices),
        sems(8 * slices),
        sems(8 * slices),
        sems(8 * slices),
        sems(row_bits + col_bits),
        sems(row_bits + col_bits),
    ]
    flops = slot_count * 6 * 2 * 3 * 2 * width * 4 * width * width
    return pl.pallas_call(
        kernel,
        out_shape=(
            jax.ShapeDtypeStruct(object_slices.shape, jnp.float32),
            jax.ShapeDtypeStruct((2, block_rows, block_cols), jnp.float32),
        ),
        in_specs=[smem] * 2 + [vmem] * 4 + [pl.BlockSpec(memory_space=pl.ANY)],
        out_specs=(vmem, vmem),
        scratch_shapes=scratch,
        compiler_params=pltpu.CompilerParams(
            vmem_limit_bytes=52 * 2**20, collective_id=0, has_side_effects=True
        ),
        cost_estimate=pl.CostEstimate(flops=flops, bytes_accessed=8 * 2**20, transcendentals=0),
    )(
        centres[0, 0], batch_order[0, 0], object_slices, probe_wave, propagator_phase,
        intensity[0, 0], jnp.asarray(np.stack(tables(width))),
    )


def solution(mesh):
    placed = (
        P(None, None, "row", "col"),
        P(),
        P(),
        P("row", "col", None, None, None),
        P("row", "col", None, None),
        P("row", "col", None),
    )
    return jax.shard_map(
        per_device,
        mesh=mesh,
        in_specs=placed,
        out_specs=(P(None, None, "row", "col"), P(None, "row", "col")),
        check_vma=False,
    )
```

```python
import math

import jax
import jax.numpy as jnp
import ml_dtypes
import numpy as np
from jax import lax
from jax.experimental import pallas as pl
from jax.experimental.pallas import tpu as pltpu
from jax.sharding import PartitionSpec as P

MESH = pl.DeviceIdType.MESH


def split(value):
    high = value.astype(jnp.bfloat16)
    low = (value - high.astype(jnp.float32)).astype(jnp.bfloat16)
    return high, low


def tables(width):
    half = width // 2
    index = np.arange(half)
    angles = (np.outer(index, index) % half) * (2.0 * math.pi / half)
    cosine = np.cos(angles) / math.sqrt(width)
    sine = np.sin(angles) / math.sqrt(width)
    out = []
    for orient in (-1.0, 1.0):
        block = np.block([[cosine, orient * sine], [-orient * sine, cosine]]).astype(np.float32)
        high = block.astype(ml_dtypes.bfloat16)
        out += [high, (block - high.astype(np.float32)).astype(ml_dtypes.bfloat16)]
    order = np.eye(width)[np.concatenate([np.arange(0, width, 2), np.arange(1, width, 2)])]
    out += [order.astype(ml_dtypes.bfloat16), order.T.astype(ml_dtypes.bfloat16)]
    turns = np.zeros((2, half + 8, width), np.float32)
    for part, values in enumerate((np.cos(index * 2.0 * math.pi / width), np.sin(index * 2.0 * math.pi / width))):
        turns[part, :half] = values[:, None]
        turns[part, half, :half] = values
    return np.stack(out), turns


def dot(left, right):
    return jnp.dot(left, right, preferred_element_type=jnp.float32)


def make_transform(table, turns, width, count):
    half = width // 2

    def right_dot(value, at):
        high, low = split(value)
        return dot(high, table[at]) + dot(low, table[at]) + dot(high, table[at + 1])

    def left_dot(value, at):
        high, low = split(value)
        return dot(table[at], high) + dot(table[at], low) + dot(table[at + 1], high)

    def along_cols(values, orient):
        re, im = values
        rows = re.shape[0]
        cosine, sine = (turns[0, half : half + 1, :half], turns[1, half : half + 1, :half])
        one, two = ((re[:, :half], im[:, :half]), (re[:, half:], im[:, half:]))
        if orient < 0:
            one, two = (one[0] + two[0], one[1] + two[1]), (one[0] - two[0], one[1] - two[1])
            two = product(two, (cosine, -sine))
        stacked = jnp.concatenate([jnp.concatenate(one, axis=1), jnp.concatenate(two, axis=1)], axis=0)
        result = right_dot(stacked, 0 if orient < 0 else 2)
        one = (result[:rows, :half], result[:rows, half:])
        two = (result[rows:, :half], result[rows:, half:])
        if orient > 0:
            two = product(two, (cosine, sine))
            one, two = (one[0] + two[0], one[1] + two[1]), (one[0] - two[0], one[1] - two[1])
        return tuple(jnp.concatenate([one[c], two[c]], axis=1) for c in range(2))

    def along_rows(values, orient):
        re, im = values
        cosine, sine = (turns[0, :half], turns[1, :half])
        pieces = []
        for slot in range(count):
            top, mid, end = (slot * width, slot * width + half, (slot + 1) * width)
            one, two = ((re[top:mid], im[top:mid]), (re[mid:end], im[mid:end]))
            if orient < 0:
                one, two = (one[0] + two[0], one[1] + two[1]), (one[0] - two[0], one[1] - two[1])
                two = product(two, (cosine, -sine))
            pieces += [jnp.concatenate(one, axis=0), jnp.concatenate(two, axis=0)]
        result = left_dot(jnp.concatenate(pieces, axis=1), 2 if orient < 0 else 0)
        parts = ([], [])
        for slot in range(count):
            left = 2 * slot * width
            one = (result[:half, left : left + width], result[half:, left : left + width])
            left += width
            two = (result[:half, left : left + width], result[half:, left : left + width])
            if orient > 0:
                two = product(two, (cosine, sine))
                one, two = (one[0] + two[0], one[1] + two[1]), (one[0] - two[0], one[1] - two[1])
            for c in range(2):
                parts[c].extend([one[c], two[c]])
        return tuple(jnp.concatenate(parts[c], axis=0) for c in range(2))

    def transform(values, orient):
        return along_rows(along_cols(values, orient), orient)

    return transform


def product(left, right):
    return (left[0] * right[0] - left[1] * right[1], left[0] * right[1] + left[1] * right[0])


def conjugate(values):
    return (values[0], -values[1])


def kernel(
    centres, live, tile, probe_hbm, phase_hbm, intensity_hbm, tables_hbm, turns_hbm, out, probe_out,
    probe, phase, intensity, table, turns, ext, acc, layer_zero, field_one, upstream_one, prop, measured,
    first_cols, first_rows, last_in, mid_cols, mid_rows,
    terms, arrived, blocks, blocks_in, table_sem,
    halo_send, halo_recv, fold_send, fold_recv, sum_send, sum_recv,
):
    slices, slot_count = tile.shape[0], intensity.shape[0]
    width = probe.shape[1]
    half = width // 2
    size = tile.shape[2] + width
    sizes = {"row": lax.axis_size("row"), "col": lax.axis_size("col")}
    at = {"row": lax.axis_index("row"), "col": lax.axis_index("col")}
    bits = {name: sizes[name].bit_length() - 1 for name in sizes}
    steps = [("row", bit) for bit in range(bits["row"])] + [("col", bit) for bit in range(bits["col"])]
    first, middle, last = pl.ds(0, half), pl.ds(half, half), pl.ds(2 * half, half)
    every = pl.ds(0, size)

    def has(axis, delta):
        return at[axis] > 0 if delta < 0 else at[axis] < sizes[axis] - 1

    def partner(axis, bit):
        odd = lax.rem(at[axis] // (1 << bit), 2)
        return odd, at[axis] + (1 - 2 * odd) * (1 << bit)

    barrier = pltpu.get_barrier_semaphore()
    count = 0
    for axis in ("row", "col"):
        for delta in (-1, 1):
            @pl.when(has(axis, delta))
            def _(axis=axis, delta=delta):
                pl.semaphore_signal(barrier, inc=1, device_id={axis: at[axis] + delta}, device_id_type=MESH)
            count = count + jnp.where(has(axis, delta), 1, 0)
    for axis, bit in steps:
        if bit > 0:
            pl.semaphore_signal(barrier, inc=1, device_id={axis: partner(axis, bit)[1]}, device_id_type=MESH)
            count = count + 1
    pl.semaphore_wait(barrier, count)

    class Shift:
        def __init__(self, src, dst, send, recv, axis, delta):
            n = sizes[axis]
            self.copy = pltpu.make_async_remote_copy(
                src_ref=src, dst_ref=dst, send_sem=send, recv_sem=recv,
                device_id={axis: lax.rem(at[axis] + delta + n, n)}, device_id_type=MESH,
            )
            self.target, self.source = has(axis, delta), has(axis, -delta)

        def start(self):
            pl.when(self.target)(lambda: self.copy.start())

        def wait_recv(self):
            pl.when(self.source)(lambda: self.copy.wait_recv())

        def wait_send(self):
            pl.when(self.target)(lambda: self.copy.wait_send())

    def halo(s, part):
        copies = []
        for side, delta in enumerate((1, -1)):
            place = first if delta > 0 else last
            for c in range(2):
                if c == 0 and part == 0:
                    src, dst, axis = tile.at[s, c], ext[s][c].at[place, middle], "row"
                elif c == 0:
                    src, dst, axis = ext[s][c].at[every, middle], ext[s][c].at[every, place], "col"
                elif part == 0:
                    src, dst, axis = tile.at[s, c], ext[s][c].at[middle, place], "col"
                else:
                    src, dst, axis = ext[s][c].at[middle, every], ext[s][c].at[place, every], "row"
                sem = ((s * 2 + part) * 2 + c) * 2 + side
                copies.append(Shift(src, dst, halo_send.at[sem], halo_recv.at[sem], axis, delta))
        return copies

    def folding(s, part):
        copies = []
        for side, delta in enumerate((1, -1)):
            place = last if delta > 0 else first
            for c in range(2):
                if c == 0 and part == 0:
                    src, dst, axis = acc[s][c].at[every, place], first_cols[s][side], "col"
                elif c == 0:
                    src, dst, axis = mid_cols[s].at[place, :], last_in[s][c][side], "row"
                elif part == 0:
                    src, dst, axis = acc[s][c].at[place, every], first_rows[s][side], "row"
                else:
                    src, dst, axis = mid_rows[s].at[:, place], last_in[s][c][side], "col"
                sem = ((s * 2 + part) * 2 + c) * 2 + side
                copies.append(Shift(src, dst, fold_send.at[sem], fold_recv.at[sem], axis, delta))
        return copies

    def start_all(copies):
        for copy in copies:
            copy.start()
        sent.extend(copies)

    def arrive_all(copies):
        for copy in copies:
            copy.wait_recv()

    sent = []
    halos = [[halo(s, part) for part in range(2)] for s in range(slices)]
    folds = [[folding(s, part) for part in range(2)] for s in range(slices)]
    for s in range(slices):
        start_all(halos[s][0])
    moves = [(tables_hbm, table), (phase_hbm, phase), (intensity_hbm, intensity), (turns_hbm, turns), (probe_hbm, probe)]
    moves += [(tile.at[s, c], ext[s][c].at[middle, middle]) for s in range(slices) for c in range(2)]
    loads = [pltpu.make_async_copy(src, dst, table_sem.at[k]) for k, (src, dst) in enumerate(moves)]
    for load in loads:
        load.start()

    for s in range(slices):
        for c in range(2):
            acc[s][c][...] = jnp.zeros((size, size), jnp.float32)
        for side, delta in enumerate((1, -1)):
            place = first if delta > 0 else last

            @pl.when(jnp.logical_not(has("row", -delta)))
            def _(s=s, side=side, place=place):
                ext[s][0][place, middle] = jnp.zeros((half, half), jnp.float32)
                ext[s][1][place, every] = jnp.zeros((half, size), jnp.float32)
                first_rows[s][side][...] = jnp.zeros((half, size), jnp.float32)
                last_in[s][0][side][...] = jnp.zeros((half, half), jnp.float32)

            @pl.when(jnp.logical_not(has("col", -delta)))
            def _(s=s, side=side, place=place):
                ext[s][1][middle, place] = jnp.zeros((half, half), jnp.float32)
                ext[s][0][every, place] = jnp.zeros((size, half), jnp.float32)
                first_cols[s][side][...] = jnp.zeros((size, half), jnp.float32)
                last_in[s][1][side][...] = jnp.zeros((half, half), jnp.float32)

    for load in loads:
        load.wait()
    for s in range(slices):
        arrive_all(halos[s][0])
        start_all(halos[s][1])

    def reordered(values):
        return dot(dot(table[4], values).astype(jnp.bfloat16), table[5])

    angles = reordered(phase[...])
    prop[0] = jnp.cos(angles)
    prop[1] = jnp.sin(angles)
    for slot in range(slot_count):
        measured[pl.ds(slot * width, width), :] = reordered(intensity[slot])
    arrive_all(halos[0][1])

    transform = make_transform(table, turns, width, slot_count)

    def start_of(slot):
        row = centres[slot, 0] - at["row"] * tile.shape[2]
        return row, centres[slot, 1] - at["col"] * tile.shape[3]

    def window(s, slot):
        row, col = start_of(slot)
        parts = []
        for c in range(2):
            band = pltpu.roll(ext[s][c][...], lax.rem(size - row, size), 0)[:width]
            parts.append(pltpu.roll(band, lax.rem(size - col, size), 1)[:, :width])
        return tuple(parts)

    def place_term(s, slot, values):
        row, col = start_of(slot)
        for c in range(2):
            wide = jnp.concatenate([values[c], jnp.zeros((width, size - width), jnp.float32)], axis=1)
            wide = pltpu.roll(wide, col, 1)
            tall = jnp.concatenate([wide, jnp.zeros((size - width, size), jnp.float32)], axis=0)
            acc[s][c][...] += pltpu.roll(tall, row, 0)

    def stack(pieces):
        return tuple(jnp.concatenate([piece[c] for piece in pieces], axis=0) for c in range(2))

    def entering_zero():
        return stack([(probe[0].astype(jnp.float32), probe[1].astype(jnp.float32))] * slot_count)

    def pair(ref):
        return (ref[0], ref[1])

    def keep(ref, values):
        ref[0] = values[0]
        ref[1] = values[1]

    def propagator():
        return stack([pair(prop)] * slot_count)

    def place_terms(s, values):
        for slot in range(slot_count):
            rows = slice(slot * width, (slot + 1) * width)
            place_term(s, slot, (values[0][rows], values[1][rows]))

    keep(layer_zero, stack([window(0, slot) for slot in range(slot_count)]))
    spectrum = transform(product(entering_zero(), pair(layer_zero)), -1.0)
    keep(field_one, transform(product(spectrum, propagator()), 1.0))
    arrive_all(halos[1][1])

    layer = stack([window(1, slot) for slot in range(slot_count)])
    spectrum = transform(product(pair(field_one), layer), -1.0)
    weights = jnp.concatenate(
        [
            jnp.full((width, width), jnp.where(live[slot] >= 0, 1.0, 0.0).astype(jnp.float32))
            for slot in range(slot_count)
        ],
        axis=0,
    )
    misfit = weights * (spectrum[0] * spectrum[0] + spectrum[1] * spectrum[1] - measured[...])
    adjoint = transform((misfit * spectrum[0], misfit * spectrum[1]), 1.0)
    place_terms(1, product(conjugate(pair(field_one)), adjoint))
    keep(upstream_one, product(conjugate(layer), adjoint))
    start_all(folds[1][0])

    def fold_middle(s):
        arrive_all(folds[s][0])
        mid_cols[s][...] = acc[s][0][every, middle] + first_cols[s][0][...] + first_cols[s][1][...]
        mid_rows[s][...] = acc[s][1][middle, every] + first_rows[s][0][...] + first_rows[s][1][...]
        start_all(folds[s][1])

    def fold_end(s):
        arrive_all(folds[s][1])
        out[s, 0] = mid_cols[s][middle, :] + last_in[s][0][0][...] + last_in[s][0][1][...]
        out[s, 1] = mid_rows[s][:, middle] + last_in[s][1][0][...] + last_in[s][1][1][...]

    spectrum = transform(pair(upstream_one), -1.0)
    fold_middle(1)
    adjoint = transform(product(spectrum, conjugate(propagator())), 1.0)
    upstream = product(conjugate(pair(layer_zero)), adjoint)
    for c in range(2):
        total = upstream[c][:width]
        for slot in range(1, slot_count):
            total = total + upstream[c][slot * width : (slot + 1) * width]
        terms[0][c] = total.reshape(terms[0].shape[1:])

    def halving(step):
        axis, bit = steps[step]
        odd, other = partner(axis, bit)
        held = terms[step] if axis == "row" else blocks[bit]
        landing = arrived[step] if axis == "row" else blocks_in[bit]
        copy = pltpu.make_async_remote_copy(
            src_ref=held.at[:, :, 1 - odd], dst_ref=landing,
            send_sem=sum_send.at[step], recv_sem=sum_recv.at[step],
            device_id={axis: other}, device_id_type=MESH,
        )
        return copy, held, landing, odd

    halvings = [halving(step) for step in range(len(steps))]

    def sum_next(step):
        copy, held, landing, odd = halvings[step]
        copy.wait()
        total = held[:, :, odd] + landing[...]
        if step + 1 == len(steps):
            probe_out[...] = total[:, 0, :, : probe_out.shape[2]]
            return
        if step + 1 < bits["row"]:
            terms[step + 1][...] = total.reshape(terms[step + 1].shape)
        elif step + 1 == bits["row"]:
            span = probe_out.shape[2]
            for j in range(sizes["col"]):
                blocks[0][:, j // 2, j % 2, :, :span] = total[:, 0, :, j * span : (j + 1) * span]
        else:
            following = blocks[step + 1 - bits["row"]]
            following[...] = total.reshape(following.shape)
        halvings[step + 1][0].start()

    if blocks[0].shape[-1] > probe_out.shape[2]:
        blocks[0][...] = jnp.zeros(blocks[0].shape, jnp.float32)
    halvings[0][0].start()

    place_terms(0, product(conjugate(entering_zero()), adjoint))
    start_all(folds[0][0])
    sum_next(0)
    fold_end(1)
    sum_next(1)
    fold_middle(0)
    for step in range(2, len(steps) - 1):
        sum_next(step)
    fold_end(0)
    sum_next(len(steps) - 1)
    for copy in sent:
        copy.wait_send()


def per_device(object_slices, probe_wave, propagator_phase, intensity, centres, batch_order):
    slices = object_slices.shape[0]
    half = object_slices.shape[2]
    width = probe_wave.shape[1]
    size = half + width
    slot_count = centres.shape[2]
    rows, cols = lax.axis_size("row"), lax.axis_size("col")
    block_rows, block_cols = width // rows, width // cols
    lanes = max(block_cols, 128)
    row_bits, col_bits = rows.bit_length() - 1, cols.bit_length() - 1
    smem = pl.BlockSpec(memory_space=pltpu.SMEM)
    vmem = pl.BlockSpec(memory_space=pltpu.VMEM)

    def floats(*shape):
        return pltpu.VMEM(shape, jnp.float32)

    def sems(count):
        return pltpu.SemaphoreType.DMA((count,))

    slot_fields = floats(2, slot_count * width, width)
    constants, twiddles = tables(width)
    scratch = [
        pltpu.VMEM(probe_wave.shape, probe_wave.dtype),
        pltpu.VMEM(propagator_phase.shape, propagator_phase.dtype),
        pltpu.VMEM(intensity.shape[2:], intensity.dtype),
        pltpu.VMEM(constants.shape, jnp.bfloat16),
        floats(*twiddles.shape),
        [[floats(size, size)] * 2] * slices,
        [[floats(size, size)] * 2] * slices,
        slot_fields,
        slot_fields,
        slot_fields,
        floats(2, width, width),
        floats(slot_count * width, width),
        [[floats(size, half)] * 2] * slices,
        [[floats(half, size)] * 2] * slices,
        [[[floats(half, half)] * 2] * 2] * slices,
        [floats(size, half)] * slices,
        [floats(half, size)] * slices,
        [floats(2, rows >> (k + 1), 2, block_rows, width) for k in range(row_bits)],
        [floats(2, rows >> (k + 1), block_rows, width) for k in range(row_bits)],
        [floats(2, cols >> (k + 1), 2, block_rows, lanes) for k in range(col_bits)],
        [floats(2, cols >> (k + 1), block_rows, lanes) for k in range(col_bits)],
        sems(5 + 2 * slices),
        sems(8 * slices),
        sems(8 * slices),
        sems(8 * slices),
        sems(8 * slices),
        sems(row_bits + col_bits),
        sems(row_bits + col_bits),
    ]
    flops = slot_count * 6 * 2 * 3 * 2 * width * 2 * width * width
    return pl.pallas_call(
        kernel,
        out_shape=(
            jax.ShapeDtypeStruct(object_slices.shape, jnp.float32),
            jax.ShapeDtypeStruct((2, block_rows, block_cols), jnp.float32),
        ),
        in_specs=[smem] * 2 + [pl.BlockSpec(memory_space=pl.ANY)] * 6,
        out_specs=(vmem, vmem),
        scratch_shapes=scratch,
        compiler_params=pltpu.CompilerParams(
            vmem_limit_bytes=60 * 2**20, collective_id=0, has_side_effects=True
        ),
        cost_estimate=pl.CostEstimate(flops=flops, bytes_accessed=8 * 2**20, transcendentals=0),
    )(
        centres[0, 0], batch_order[0, 0], object_slices, probe_wave, propagator_phase,
        intensity[0, 0], jnp.asarray(constants), jnp.asarray(twiddles),
    )


def solution(mesh):
    placed = (
        P(None, None, "row", "col"),
        P(),
        P(),
        P("row", "col", None, None, None),
        P("row", "col", None, None),
        P("row", "col", None),
    )
    return jax.shard_map(
        per_device,
        mesh=mesh,
        in_specs=placed,
        out_specs=(P(None, None, "row", "col"), P(None, "row", "col")),
        check_vma=False,
    )
```

```python
import math

import jax
import jax.numpy as jnp
import ml_dtypes
import numpy as np
from jax import lax
from jax.experimental import pallas as pl
from jax.experimental.pallas import tpu as pltpu
from jax.sharding import PartitionSpec as P

MESH = pl.DeviceIdType.MESH


def split(value):
    high = value.astype(jnp.bfloat16)
    low = (value - high.astype(jnp.float32)).astype(jnp.bfloat16)
    return high, low


def tables(width):
    half = width // 2
    index = np.arange(half)
    angles = (np.outer(index, index) % half) * (2.0 * math.pi / half)
    cosine = np.cos(angles) / math.sqrt(width)
    sine = np.sin(angles) / math.sqrt(width)
    out = []
    for orient in (-1.0, 1.0):
        block = np.block([[cosine, orient * sine], [-orient * sine, cosine]]).astype(np.float32)
        high = block.astype(ml_dtypes.bfloat16)
        out += [high, (block - high.astype(np.float32)).astype(ml_dtypes.bfloat16)]
    order = np.eye(width)[np.concatenate([np.arange(0, width, 2), np.arange(1, width, 2)])]
    out += [order.astype(ml_dtypes.bfloat16), order.T.astype(ml_dtypes.bfloat16)]
    turns = np.zeros((2, half + 8, width), np.float32)
    for part, values in enumerate((np.cos(index * 2.0 * math.pi / width), np.sin(index * 2.0 * math.pi / width))):
        turns[part, :half] = values[:, None]
        turns[part, half, :half] = values
    return np.stack(out), turns


def dot(left, right):
    return jnp.dot(left, right, preferred_element_type=jnp.float32)


def make_transform(table, turns, width, count):
    half = width // 2

    def right_dot(value, at):
        high, low = split(value)
        return dot(high, table[at]) + dot(low, table[at]) + dot(high, table[at + 1])

    def left_dot(value, at):
        high, low = split(value)
        return dot(table[at], high) + dot(table[at], low) + dot(table[at + 1], high)

    def along_cols(values, orient):
        re, im = values
        rows = re.shape[0]
        cosine, sine = (turns[0, half : half + 1, :half], turns[1, half : half + 1, :half])
        one, two = ((re[:, :half], im[:, :half]), (re[:, half:], im[:, half:]))
        if orient < 0:
            one, two = (one[0] + two[0], one[1] + two[1]), (one[0] - two[0], one[1] - two[1])
            two = product(two, (cosine, -sine))
        stacked = jnp.concatenate([jnp.concatenate(one, axis=1), jnp.concatenate(two, axis=1)], axis=0)
        result = right_dot(stacked, 0 if orient < 0 else 2)
        one = (result[:rows, :half], result[:rows, half:])
        two = (result[rows:, :half], result[rows:, half:])
        if orient > 0:
            two = product(two, (cosine, sine))
            one, two = (one[0] + two[0], one[1] + two[1]), (one[0] - two[0], one[1] - two[1])
        return tuple(jnp.concatenate([one[c], two[c]], axis=1) for c in range(2))

    def along_rows(values, orient):
        re, im = values
        cosine, sine = (turns[0, :half], turns[1, :half])
        pieces = []
        for slot in range(count):
            top, mid, end = (slot * width, slot * width + half, (slot + 1) * width)
            one, two = ((re[top:mid], im[top:mid]), (re[mid:end], im[mid:end]))
            if orient < 0:
                one, two = (one[0] + two[0], one[1] + two[1]), (one[0] - two[0], one[1] - two[1])
                two = product(two, (cosine, -sine))
            pieces += [jnp.concatenate(one, axis=0), jnp.concatenate(two, axis=0)]
        result = left_dot(jnp.concatenate(pieces, axis=1), 2 if orient < 0 else 0)
        parts = ([], [])
        for slot in range(count):
            left = 2 * slot * width
            one = (result[:half, left : left + width], result[half:, left : left + width])
            left += width
            two = (result[:half, left : left + width], result[half:, left : left + width])
            if orient > 0:
                two = product(two, (cosine, sine))
                one, two = (one[0] + two[0], one[1] + two[1]), (one[0] - two[0], one[1] - two[1])
            for c in range(2):
                parts[c].extend([one[c], two[c]])
        return tuple(jnp.concatenate(parts[c], axis=0) for c in range(2))

    def transform(values, orient):
        return along_rows(along_cols(values, orient), orient)

    return transform


def product(left, right):
    return (left[0] * right[0] - left[1] * right[1], left[0] * right[1] + left[1] * right[0])


def conjugate(values):
    return (values[0], -values[1])


def kernel(
    centres, live, tile, probe_hbm, phase_hbm, intensity_hbm, tables_hbm, turns_hbm, out, probe_out,
    probe, phase, intensity, table, turns, ext, acc, layer_zero, field_one, upstream_one, prop, measured,
    first_cols, first_rows, last_in, mid_cols, mid_rows,
    terms, arrived, blocks, blocks_in, table_sem,
    halo_send, halo_recv, fold_send, fold_recv, sum_send, sum_recv,
):
    slices, slot_count = tile.shape[0], intensity.shape[0]
    width = probe.shape[1]
    half = width // 2
    size = tile.shape[2] + width
    sizes = {"row": lax.axis_size("row"), "col": lax.axis_size("col")}
    at = {"row": lax.axis_index("row"), "col": lax.axis_index("col")}
    bits = {name: sizes[name].bit_length() - 1 for name in sizes}
    steps = [("row", bit) for bit in range(bits["row"])] + [("col", bit) for bit in range(bits["col"])]
    first, middle, last = pl.ds(0, half), pl.ds(half, half), pl.ds(2 * half, half)
    every = pl.ds(0, size)

    def has(axis, delta):
        return at[axis] > 0 if delta < 0 else at[axis] < sizes[axis] - 1

    def partner(axis, bit):
        odd = lax.rem(at[axis] // (1 << bit), 2)
        return odd, at[axis] + (1 - 2 * odd) * (1 << bit)

    barrier = pltpu.get_barrier_semaphore()
    count = 0
    for axis in ("row", "col"):
        for delta in (-1, 1):
            @pl.when(has(axis, delta))
            def _(axis=axis, delta=delta):
                pl.semaphore_signal(barrier, inc=1, device_id={axis: at[axis] + delta}, device_id_type=MESH)
            count = count + jnp.where(has(axis, delta), 1, 0)
    for axis, bit in steps:
        if bit > 0:
            pl.semaphore_signal(barrier, inc=1, device_id={axis: partner(axis, bit)[1]}, device_id_type=MESH)
            count = count + 1

    moves = [(tables_hbm, table), (phase_hbm, phase), (intensity_hbm, intensity), (turns_hbm, turns), (probe_hbm, probe)]
    moves += [(tile.at[s, c], ext[s][c].at[middle, middle]) for s in range(slices) for c in range(2)]
    loads = [pltpu.make_async_copy(src, dst, table_sem.at[k]) for k, (src, dst) in enumerate(moves)]
    for load in loads:
        load.start()

    for s in range(slices):
        for side, delta in enumerate((1, -1)):
            place = first if delta > 0 else last

            @pl.when(jnp.logical_not(has("row", -delta)))
            def _(s=s, side=side, place=place):
                ext[s][0][place, middle] = jnp.zeros((half, half), jnp.float32)
                ext[s][1][place, every] = jnp.zeros((half, size), jnp.float32)
                first_rows[s][side][...] = jnp.zeros((half, size), jnp.float32)
                last_in[s][0][side][...] = jnp.zeros((half, half), jnp.float32)

            @pl.when(jnp.logical_not(has("col", -delta)))
            def _(s=s, side=side, place=place):
                ext[s][1][middle, place] = jnp.zeros((half, half), jnp.float32)
                ext[s][0][every, place] = jnp.zeros((size, half), jnp.float32)
                first_cols[s][side][...] = jnp.zeros((size, half), jnp.float32)
                last_in[s][1][side][...] = jnp.zeros((half, half), jnp.float32)
    pl.semaphore_wait(barrier, count)

    class Shift:
        def __init__(self, src, dst, send, recv, axis, delta):
            n = sizes[axis]
            self.copy = pltpu.make_async_remote_copy(
                src_ref=src, dst_ref=dst, send_sem=send, recv_sem=recv,
                device_id={axis: lax.rem(at[axis] + delta + n, n)}, device_id_type=MESH,
            )
            self.target, self.source = has(axis, delta), has(axis, -delta)

        def start(self):
            pl.when(self.target)(lambda: self.copy.start())

        def wait_recv(self):
            pl.when(self.source)(lambda: self.copy.wait_recv())

        def wait_send(self):
            pl.when(self.target)(lambda: self.copy.wait_send())

    def halo(s, part):
        copies = []
        for side, delta in enumerate((1, -1)):
            place = first if delta > 0 else last
            for c in range(2):
                if c == 0 and part == 0:
                    src, dst, axis = tile.at[s, c], ext[s][c].at[place, middle], "row"
                elif c == 0:
                    src, dst, axis = ext[s][c].at[every, middle], ext[s][c].at[every, place], "col"
                elif part == 0:
                    src, dst, axis = tile.at[s, c], ext[s][c].at[middle, place], "col"
                else:
                    src, dst, axis = ext[s][c].at[middle, every], ext[s][c].at[place, every], "row"
                sem = ((s * 2 + part) * 2 + c) * 2 + side
                copies.append(Shift(src, dst, halo_send.at[sem], halo_recv.at[sem], axis, delta))
        return copies

    def folding(s, part):
        copies = []
        for side, delta in enumerate((1, -1)):
            place = last if delta > 0 else first
            for c in range(2):
                if c == 0 and part == 0:
                    src, dst, axis = acc[s][c].at[every, place], first_cols[s][side], "col"
                elif c == 0:
                    src, dst, axis = mid_cols[s].at[place, :], last_in[s][c][side], "row"
                elif part == 0:
                    src, dst, axis = acc[s][c].at[place, every], first_rows[s][side], "row"
                else:
                    src, dst, axis = mid_rows[s].at[:, place], last_in[s][c][side], "col"
                sem = ((s * 2 + part) * 2 + c) * 2 + side
                copies.append(Shift(src, dst, fold_send.at[sem], fold_recv.at[sem], axis, delta))
        return copies

    def start_all(copies):
        for copy in copies:
            copy.start()
        sent.extend(copies)

    def arrive_all(copies):
        for copy in copies:
            copy.wait_recv()

    sent = []
    halos = [[halo(s, part) for part in range(2)] for s in range(slices)]
    folds = [[folding(s, part) for part in range(2)] for s in range(slices)]
    for s in range(slices):
        start_all(halos[s][0])
    for load in loads:
        load.wait()
    arrive_all(halos[0][0])
    start_all(halos[0][1])

    def reordered(values):
        return dot(dot(table[4], values).astype(jnp.bfloat16), table[5])

    angles = reordered(phase[...])
    prop[0] = jnp.cos(angles)
    prop[1] = jnp.sin(angles)
    for slot in range(slot_count):
        measured[pl.ds(slot * width, width), :] = reordered(intensity[slot])
    arrive_all(halos[0][1])
    for s in range(1, slices):
        arrive_all(halos[s][0])
        start_all(halos[s][1])

    transform = make_transform(table, turns, width, slot_count)

    def start_of(slot):
        row = centres[slot, 0] - at["row"] * tile.shape[2]
        return row, centres[slot, 1] - at["col"] * tile.shape[3]

    def window(s, slot):
        row, col = start_of(slot)
        parts = []
        for c in range(2):
            band = pltpu.roll(ext[s][c][...], lax.rem(size - row, size), 0)[:width]
            parts.append(pltpu.roll(band, lax.rem(size - col, size), 1)[:, :width])
        return tuple(parts)

    def place_terms(s, values):
        for c in range(2):
            total = None
            for slot in range(slot_count):
                row, col = start_of(slot)
                value = values[c][slot * width : (slot + 1) * width]
                wide = jnp.concatenate([value, jnp.zeros((width, size - width), jnp.float32)], axis=1)
                wide = pltpu.roll(wide, col, 1)
                tall = jnp.concatenate([wide, jnp.zeros((size - width, size), jnp.float32)], axis=0)
                tall = pltpu.roll(tall, row, 0)
                total = tall if total is None else total + tall
            acc[s][c][...] = total
            start_all(folds[s][0][c::2])

    def stack(pieces):
        return tuple(jnp.concatenate([piece[c] for piece in pieces], axis=0) for c in range(2))

    def entering_zero():
        return stack([(probe[0].astype(jnp.float32), probe[1].astype(jnp.float32))] * slot_count)

    def pair(ref):
        return (ref[0], ref[1])

    def keep(ref, values):
        ref[0] = values[0]
        ref[1] = values[1]

    def propagator():
        return stack([pair(prop)] * slot_count)

    keep(layer_zero, stack([window(0, slot) for slot in range(slot_count)]))
    spectrum = transform(product(entering_zero(), pair(layer_zero)), -1.0)
    keep(field_one, transform(product(spectrum, propagator()), 1.0))
    arrive_all(halos[1][1])

    layer = stack([window(1, slot) for slot in range(slot_count)])
    spectrum = transform(product(pair(field_one), layer), -1.0)
    weights = jnp.concatenate(
        [
            jnp.full((width, width), jnp.where(live[slot] >= 0, 1.0, 0.0).astype(jnp.float32))
            for slot in range(slot_count)
        ],
        axis=0,
    )
    misfit = weights * (spectrum[0] * spectrum[0] + spectrum[1] * spectrum[1] - measured[...])
    adjoint = transform((misfit * spectrum[0], misfit * spectrum[1]), 1.0)
    place_terms(1, product(conjugate(pair(field_one)), adjoint))
    keep(upstream_one, product(conjugate(layer), adjoint))

    def fold_middle(s):
        arrive_all(folds[s][0])
        mid_cols[s][...] = acc[s][0][every, middle] + first_cols[s][0][...] + first_cols[s][1][...]
        mid_rows[s][...] = acc[s][1][middle, every] + first_rows[s][0][...] + first_rows[s][1][...]
        start_all(folds[s][1])

    def fold_end(s):
        arrive_all(folds[s][1])
        out[s, 0] = mid_cols[s][middle, :] + last_in[s][0][0][...] + last_in[s][0][1][...]
        out[s, 1] = mid_rows[s][:, middle] + last_in[s][1][0][...] + last_in[s][1][1][...]

    spectrum = transform(pair(upstream_one), -1.0)
    fold_middle(1)
    adjoint = transform(product(spectrum, conjugate(propagator())), 1.0)
    upstream = product(conjugate(pair(layer_zero)), adjoint)
    for c in range(2):
        total = upstream[c][:width]
        for slot in range(1, slot_count):
            total = total + upstream[c][slot * width : (slot + 1) * width]
        terms[0][c] = total.reshape(terms[0].shape[1:])

    def halving(step):
        axis, bit = steps[step]
        odd, other = partner(axis, bit)
        held = terms[step] if axis == "row" else blocks[bit]
        landing = arrived[step] if axis == "row" else blocks_in[bit]
        copy = pltpu.make_async_remote_copy(
            src_ref=held.at[:, :, 1 - odd], dst_ref=landing,
            send_sem=sum_send.at[step], recv_sem=sum_recv.at[step],
            device_id={axis: other}, device_id_type=MESH,
        )
        return copy, held, landing, odd

    halvings = [halving(step) for step in range(len(steps))]

    def sum_next(step):
        copy, held, landing, odd = halvings[step]
        copy.wait()
        total = held[:, :, odd] + landing[...]
        if step + 1 == len(steps):
            probe_out[...] = total[:, 0, :, : probe_out.shape[2]]
            return
        if step + 1 < bits["row"]:
            terms[step + 1][...] = total.reshape(terms[step + 1].shape)
        elif step + 1 == bits["row"]:
            span = probe_out.shape[2]
            for j in range(sizes["col"]):
                blocks[0][:, j // 2, j % 2, :, :span] = total[:, 0, :, j * span : (j + 1) * span]
        else:
            following = blocks[step + 1 - bits["row"]]
            following[...] = total.reshape(following.shape)
        halvings[step + 1][0].start()

    if blocks[0].shape[-1] > probe_out.shape[2]:
        blocks[0][...] = jnp.zeros(blocks[0].shape, jnp.float32)
    halvings[0][0].start()

    place_terms(0, product(conjugate(entering_zero()), adjoint))
    sum_next(0)
    fold_end(1)
    sum_next(1)
    fold_middle(0)
    for step in range(2, len(steps) - 1):
        sum_next(step)
    fold_end(0)
    sum_next(len(steps) - 1)
    for copy in sent:
        copy.wait_send()


def per_device(object_slices, probe_wave, propagator_phase, intensity, centres, batch_order):
    slices = object_slices.shape[0]
    half = object_slices.shape[2]
    width = probe_wave.shape[1]
    size = half + width
    slot_count = centres.shape[2]
    rows, cols = lax.axis_size("row"), lax.axis_size("col")
    block_rows, block_cols = width // rows, width // cols
    lanes = max(block_cols, 128)
    row_bits, col_bits = rows.bit_length() - 1, cols.bit_length() - 1
    smem = pl.BlockSpec(memory_space=pltpu.SMEM)
    vmem = pl.BlockSpec(memory_space=pltpu.VMEM)

    def floats(*shape):
        return pltpu.VMEM(shape, jnp.float32)

    def sems(count):
        return pltpu.SemaphoreType.DMA((count,))

    slot_fields = floats(2, slot_count * width, width)
    constants, twiddles = tables(width)
    scratch = [
        pltpu.VMEM(probe_wave.shape, probe_wave.dtype),
        pltpu.VMEM(propagator_phase.shape, propagator_phase.dtype),
        pltpu.VMEM(intensity.shape[2:], intensity.dtype),
        pltpu.VMEM(constants.shape, jnp.bfloat16),
        floats(*twiddles.shape),
        [[floats(size, size)] * 2] * slices,
        [[floats(size, size)] * 2] * slices,
        slot_fields,
        slot_fields,
        slot_fields,
        floats(2, width, width),
        floats(slot_count * width, width),
        [[floats(size, half)] * 2] * slices,
        [[floats(half, size)] * 2] * slices,
        [[[floats(half, half)] * 2] * 2] * slices,
        [floats(size, half)] * slices,
        [floats(half, size)] * slices,
        [floats(2, rows >> (k + 1), 2, block_rows, width) for k in range(row_bits)],
        [floats(2, rows >> (k + 1), block_rows, width) for k in range(row_bits)],
        [floats(2, cols >> (k + 1), 2, block_rows, lanes) for k in range(col_bits)],
        [floats(2, cols >> (k + 1), block_rows, lanes) for k in range(col_bits)],
        sems(5 + 2 * slices),
        sems(8 * slices),
        sems(8 * slices),
        sems(8 * slices),
        sems(8 * slices),
        sems(row_bits + col_bits),
        sems(row_bits + col_bits),
    ]
    flops = slot_count * 6 * 2 * 3 * 2 * width * 2 * width * width
    return pl.pallas_call(
        kernel,
        out_shape=(
            jax.ShapeDtypeStruct(object_slices.shape, jnp.float32),
            jax.ShapeDtypeStruct((2, block_rows, block_cols), jnp.float32),
        ),
        in_specs=[smem] * 2 + [pl.BlockSpec(memory_space=pl.ANY)] * 6,
        out_specs=(vmem, vmem),
        scratch_shapes=scratch,
        compiler_params=pltpu.CompilerParams(
            vmem_limit_bytes=60 * 2**20, collective_id=0, has_side_effects=True
        ),
        cost_estimate=pl.CostEstimate(flops=flops, bytes_accessed=8 * 2**20, transcendentals=0),
    )(
        centres[0, 0], batch_order[0, 0], object_slices, probe_wave, propagator_phase,
        intensity[0, 0], jnp.asarray(constants), jnp.asarray(twiddles),
    )


def solution(mesh):
    placed = (
        P(None, None, "row", "col"),
        P(),
        P(),
        P("row", "col", None, None, None),
        P("row", "col", None, None),
        P("row", "col", None),
    )
    return jax.shard_map(
        per_device,
        mesh=mesh,
        in_specs=placed,
        out_specs=(P(None, None, "row", "col"), P(None, "row", "col")),
        check_vma=False,
    )
```

```python
import math

import jax
import jax.numpy as jnp
import ml_dtypes
import numpy as np
from jax import lax
from jax.experimental import pallas as pl
from jax.experimental.pallas import tpu as pltpu
from jax.sharding import PartitionSpec as P

MESH = pl.DeviceIdType.MESH


def split(value):
    high = value.astype(jnp.bfloat16)
    low = (value - high.astype(jnp.float32)).astype(jnp.bfloat16)
    return high, low


def tables(width):
    half = width // 2
    index = np.arange(half)
    angles = (np.outer(index, index) % half) * (2.0 * math.pi / half)
    cosine = np.cos(angles) / math.sqrt(width)
    sine = np.sin(angles) / math.sqrt(width)
    out = []
    for orient in (-1.0, 1.0):
        block = np.block([[cosine, orient * sine], [-orient * sine, cosine]]).astype(np.float32)
        high = block.astype(ml_dtypes.bfloat16)
        out += [high, (block - high.astype(np.float32)).astype(ml_dtypes.bfloat16)]
    order = np.eye(width)[np.concatenate([np.arange(0, width, 2), np.arange(1, width, 2)])]
    out += [order.astype(ml_dtypes.bfloat16), order.T.astype(ml_dtypes.bfloat16)]
    turns = np.zeros((2, half + 8, width), np.float32)
    for part, values in enumerate((np.cos(index * 2.0 * math.pi / width), np.sin(index * 2.0 * math.pi / width))):
        turns[part, :half] = values[:, None]
        turns[part, half, :half] = values
    return np.stack(out), turns


def dot(left, right):
    return jnp.dot(left, right, preferred_element_type=jnp.float32)


def make_transform(table, turns, width, count):
    half = width // 2

    def right_dot(value, at):
        high, low = split(value)
        return dot(high, table[at]) + dot(low, table[at]) + dot(high, table[at + 1])

    def left_dot(value, at):
        high, low = split(value)
        return dot(table[at], high) + dot(table[at], low) + dot(table[at + 1], high)

    def along_cols(values, orient):
        re, im = values
        rows = re.shape[0]
        cosine, sine = (turns[0, half : half + 1, :half], turns[1, half : half + 1, :half])
        one, two = ((re[:, :half], im[:, :half]), (re[:, half:], im[:, half:]))
        if orient < 0:
            one, two = (one[0] + two[0], one[1] + two[1]), (one[0] - two[0], one[1] - two[1])
            two = product(two, (cosine, -sine))
        stacked = jnp.concatenate([jnp.concatenate(one, axis=1), jnp.concatenate(two, axis=1)], axis=0)
        result = right_dot(stacked, 0 if orient < 0 else 2)
        one = (result[:rows, :half], result[:rows, half:])
        two = (result[rows:, :half], result[rows:, half:])
        if orient > 0:
            two = product(two, (cosine, sine))
            one, two = (one[0] + two[0], one[1] + two[1]), (one[0] - two[0], one[1] - two[1])
        return tuple(jnp.concatenate([one[c], two[c]], axis=1) for c in range(2))

    def along_rows(values, orient):
        re, im = values
        cosine, sine = (turns[0, :half], turns[1, :half])
        pieces = []
        for slot in range(count):
            top, mid, end = (slot * width, slot * width + half, (slot + 1) * width)
            one, two = ((re[top:mid], im[top:mid]), (re[mid:end], im[mid:end]))
            if orient < 0:
                one, two = (one[0] + two[0], one[1] + two[1]), (one[0] - two[0], one[1] - two[1])
                two = product(two, (cosine, -sine))
            pieces += [jnp.concatenate(one, axis=0), jnp.concatenate(two, axis=0)]
        result = left_dot(jnp.concatenate(pieces, axis=1), 2 if orient < 0 else 0)
        parts = ([], [])
        for slot in range(count):
            left = 2 * slot * width
            one = (result[:half, left : left + width], result[half:, left : left + width])
            left += width
            two = (result[:half, left : left + width], result[half:, left : left + width])
            if orient > 0:
                two = product(two, (cosine, sine))
                one, two = (one[0] + two[0], one[1] + two[1]), (one[0] - two[0], one[1] - two[1])
            for c in range(2):
                parts[c].extend([one[c], two[c]])
        return tuple(jnp.concatenate(parts[c], axis=0) for c in range(2))

    def transform(values, orient):
        return along_rows(along_cols(values, orient), orient)

    return transform


def product(left, right):
    return (left[0] * right[0] - left[1] * right[1], left[0] * right[1] + left[1] * right[0])


def conjugate(values):
    return (values[0], -values[1])


def kernel(
    centres, live, tile, probe_hbm, phase_hbm, intensity_hbm, tables_hbm, turns_hbm, out, probe_out,
    probe, phase, intensity, table, turns, ext, acc, layer_zero, field_one, upstream_one, prop, measured,
    first_cols, first_rows, last_in, mid_cols, mid_rows,
    terms, arrived, blocks, blocks_in, table_sem,
    halo_send, halo_recv, fold_send, fold_recv, sum_send, sum_recv,
):
    slices, slot_count = tile.shape[0], intensity.shape[0]
    width = probe.shape[1]
    half = width // 2
    size = tile.shape[2] + width
    sizes = {"row": lax.axis_size("row"), "col": lax.axis_size("col")}
    at = {"row": lax.axis_index("row"), "col": lax.axis_index("col")}
    bits = {name: sizes[name].bit_length() - 1 for name in sizes}
    steps = [("row", bit) for bit in range(bits["row"])] + [("col", bit) for bit in range(bits["col"])]
    first, middle, last = pl.ds(0, half), pl.ds(half, half), pl.ds(2 * half, half)
    every = pl.ds(0, size)

    def has(axis, delta):
        return at[axis] > 0 if delta < 0 else at[axis] < sizes[axis] - 1

    def partner(axis, bit):
        odd = lax.rem(at[axis] // (1 << bit), 2)
        return odd, at[axis] + (1 - 2 * odd) * (1 << bit)

    barrier = pltpu.get_barrier_semaphore()
    count = 0
    for axis in ("row", "col"):
        for delta in (-1, 1):
            @pl.when(has(axis, delta))
            def _(axis=axis, delta=delta):
                pl.semaphore_signal(barrier, inc=1, device_id={axis: at[axis] + delta}, device_id_type=MESH)
            count = count + jnp.where(has(axis, delta), 1, 0)
    for axis, bit in steps:
        if bit > 0:
            pl.semaphore_signal(barrier, inc=1, device_id={axis: partner(axis, bit)[1]}, device_id_type=MESH)
            count = count + 1

    moves = [(tables_hbm, table), (phase_hbm, phase), (intensity_hbm, intensity), (turns_hbm, turns), (probe_hbm, probe)]
    moves += [(tile.at[s, c], ext[s][c].at[middle, middle]) for s in range(slices) for c in range(2)]
    loads = [pltpu.make_async_copy(src, dst, table_sem.at[k]) for k, (src, dst) in enumerate(moves)]
    for load in loads:
        load.start()

    for s in range(slices):
        for side, delta in enumerate((1, -1)):
            place = first if delta > 0 else last

            @pl.when(jnp.logical_not(has("row", -delta)))
            def _(s=s, side=side, place=place):
                ext[s][0][place, middle] = jnp.zeros((half, half), jnp.float32)
                ext[s][1][place, every] = jnp.zeros((half, size), jnp.float32)
                first_rows[s][side][...] = jnp.zeros((half, size), jnp.float32)
                last_in[s][0][side][...] = jnp.zeros((half, half), jnp.float32)

            @pl.when(jnp.logical_not(has("col", -delta)))
            def _(s=s, side=side, place=place):
                ext[s][1][middle, place] = jnp.zeros((half, half), jnp.float32)
                ext[s][0][every, place] = jnp.zeros((size, half), jnp.float32)
                first_cols[s][side][...] = jnp.zeros((size, half), jnp.float32)
                last_in[s][1][side][...] = jnp.zeros((half, half), jnp.float32)
    pl.semaphore_wait(barrier, count)

    class Shift:
        def __init__(self, src, dst, send, recv, axis, delta):
            n = sizes[axis]
            self.copy = pltpu.make_async_remote_copy(
                src_ref=src, dst_ref=dst, send_sem=send, recv_sem=recv,
                device_id={axis: lax.rem(at[axis] + delta + n, n)}, device_id_type=MESH,
            )
            self.target, self.source = has(axis, delta), has(axis, -delta)

        def start(self):
            pl.when(self.target)(lambda: self.copy.start())

        def wait_recv(self):
            pl.when(self.source)(lambda: self.copy.wait_recv())

        def wait_send(self):
            pl.when(self.target)(lambda: self.copy.wait_send())

    def halo(s, part):
        copies = []
        for side, delta in enumerate((1, -1)):
            place = first if delta > 0 else last
            for c in range(2):
                if c == 0 and part == 0:
                    src, dst, axis = tile.at[s, c], ext[s][c].at[place, middle], "row"
                elif c == 0:
                    src, dst, axis = ext[s][c].at[every, middle], ext[s][c].at[every, place], "col"
                elif part == 0:
                    src, dst, axis = tile.at[s, c], ext[s][c].at[middle, place], "col"
                else:
                    src, dst, axis = ext[s][c].at[middle, every], ext[s][c].at[place, every], "row"
                sem = ((s * 2 + part) * 2 + c) * 2 + side
                copies.append(Shift(src, dst, halo_send.at[sem], halo_recv.at[sem], axis, delta))
        return copies

    def folding(s, part):
        copies = []
        for side, delta in enumerate((1, -1)):
            place = last if delta > 0 else first
            for c in range(2):
                if c == 0 and part == 0:
                    src, dst, axis = acc[s][c].at[every, place], first_cols[s][side], "col"
                elif c == 0:
                    src, dst, axis = mid_cols[s].at[place, :], last_in[s][c][side], "row"
                elif part == 0:
                    src, dst, axis = acc[s][c].at[place, every], first_rows[s][side], "row"
                else:
                    src, dst, axis = mid_rows[s].at[:, place], last_in[s][c][side], "col"
                sem = ((s * 2 + part) * 2 + c) * 2 + side
                copies.append(Shift(src, dst, fold_send.at[sem], fold_recv.at[sem], axis, delta))
        return copies

    def start_all(copies):
        for copy in copies:
            copy.start()
        sent.extend(copies)

    def arrive_all(copies):
        for copy in copies:
            copy.wait_recv()

    sent = []
    halos = [[halo(s, part) for part in range(2)] for s in range(slices)]
    folds = [[folding(s, part) for part in range(2)] for s in range(slices)]
    for s in range(slices):
        start_all(halos[s][0])
    for load in loads:
        load.wait()
    for s in range(slices):
        arrive_all(halos[s][0])
        start_all(halos[s][1])

    def reordered(values):
        return dot(dot(table[4], values).astype(jnp.bfloat16), table[5])

    angles = reordered(phase[...])
    prop[0] = jnp.cos(angles)
    prop[1] = jnp.sin(angles)
    for slot in range(slot_count):
        measured[pl.ds(slot * width, width), :] = reordered(intensity[slot])
    arrive_all(halos[0][1])

    transform = make_transform(table, turns, width, slot_count)

    def start_of(slot):
        row = centres[slot, 0] - at["row"] * tile.shape[2]
        return row, centres[slot, 1] - at["col"] * tile.shape[3]

    def window(s, slot):
        row, col = start_of(slot)
        parts = []
        for c in range(2):
            band = pltpu.roll(ext[s][c][...], lax.rem(size - row, size), 0)[:width]
            parts.append(pltpu.roll(band, lax.rem(size - col, size), 1)[:, :width])
        return tuple(parts)

    def place_terms(s, values):
        for c in range(2):
            total = None
            for slot in range(slot_count):
                row, col = start_of(slot)
                value = values[c][slot * width : (slot + 1) * width]
                wide = jnp.concatenate([value, jnp.zeros((width, size - width), jnp.float32)], axis=1)
                wide = pltpu.roll(wide, col, 1)
                tall = jnp.concatenate([wide, jnp.zeros((size - width, size), jnp.float32)], axis=0)
                tall = pltpu.roll(tall, row, 0)
                total = tall if total is None else total + tall
            acc[s][c][...] = total
            start_all(folds[s][0][c::2])

    def stack(pieces):
        return tuple(jnp.concatenate([piece[c] for piece in pieces], axis=0) for c in range(2))

    def entering_zero():
        return stack([(probe[0].astype(jnp.float32), probe[1].astype(jnp.float32))] * slot_count)

    def pair(ref):
        return (ref[0], ref[1])

    def keep(ref, values):
        ref[0] = values[0]
        ref[1] = values[1]

    def propagator():
        return stack([pair(prop)] * slot_count)

    keep(layer_zero, stack([window(0, slot) for slot in range(slot_count)]))
    spectrum = transform(product(entering_zero(), pair(layer_zero)), -1.0)
    keep(field_one, transform(product(spectrum, propagator()), 1.0))
    arrive_all(halos[1][1])

    layer = stack([window(1, slot) for slot in range(slot_count)])
    spectrum = transform(product(pair(field_one), layer), -1.0)
    weights = jnp.concatenate(
        [
            jnp.full((width, width), jnp.where(live[slot] >= 0, 1.0, 0.0).astype(jnp.float32))
            for slot in range(slot_count)
        ],
        axis=0,
    )
    misfit = weights * (spectrum[0] * spectrum[0] + spectrum[1] * spectrum[1] - measured[...])
    adjoint = transform((misfit * spectrum[0], misfit * spectrum[1]), 1.0)
    place_terms(1, product(conjugate(pair(field_one)), adjoint))
    keep(upstream_one, product(conjugate(layer), adjoint))

    def fold_middle(s):
        arrive_all(folds[s][0])
        mid_cols[s][...] = acc[s][0][every, middle] + first_cols[s][0][...] + first_cols[s][1][...]
        mid_rows[s][...] = acc[s][1][middle, every] + first_rows[s][0][...] + first_rows[s][1][...]
        start_all(folds[s][1])

    def fold_end(s):
        arrive_all(folds[s][1])
        out[s, 0] = mid_cols[s][middle, :] + last_in[s][0][0][...] + last_in[s][0][1][...]
        out[s, 1] = mid_rows[s][:, middle] + last_in[s][1][0][...] + last_in[s][1][1][...]

    spectrum = transform(pair(upstream_one), -1.0)
    fold_middle(1)
    adjoint = transform(product(spectrum, conjugate(propagator())), 1.0)
    upstream = product(conjugate(pair(layer_zero)), adjoint)
    for c in range(2):
        total = upstream[c][:width]
        for slot in range(1, slot_count):
            total = total + upstream[c][slot * width : (slot + 1) * width]
        terms[0][c] = total.reshape(terms[0].shape[1:])

    def halving(step):
        axis, bit = steps[step]
        odd, other = partner(axis, bit)
        held = terms[step] if axis == "row" else blocks[bit]
        landing = arrived[step] if axis == "row" else blocks_in[bit]
        copy = pltpu.make_async_remote_copy(
            src_ref=held.at[:, :, 1 - odd], dst_ref=landing,
            send_sem=sum_send.at[step], recv_sem=sum_recv.at[step],
            device_id={axis: other}, device_id_type=MESH,
        )
        return copy, held, landing, odd

    halvings = [halving(step) for step in range(len(steps))]

    def sum_next(step):
        copy, held, landing, odd = halvings[step]
        copy.wait()
        total = held[:, :, odd] + landing[...]
        if step + 1 == len(steps):
            probe_out[...] = total[:, 0, :, : probe_out.shape[2]]
            return
        if step + 1 < bits["row"]:
            terms[step + 1][...] = total.reshape(terms[step + 1].shape)
        elif step + 1 == bits["row"]:
            span = probe_out.shape[2]
            for j in range(sizes["col"]):
                blocks[0][:, j // 2, j % 2, :, :span] = total[:, 0, :, j * span : (j + 1) * span]
        else:
            following = blocks[step + 1 - bits["row"]]
            following[...] = total.reshape(following.shape)
        halvings[step + 1][0].start()

    if blocks[0].shape[-1] > probe_out.shape[2]:
        blocks[0][...] = jnp.zeros(blocks[0].shape, jnp.float32)
    halvings[0][0].start()

    place_terms(0, product(conjugate(entering_zero()), adjoint))
    sum_next(0)
    fold_end(1)
    sum_next(1)
    fold_middle(0)
    for step in range(2, len(steps) - 1):
        sum_next(step)
    fold_end(0)
    sum_next(len(steps) - 1)
    for copy in sent:
        copy.wait_send()


def per_device(object_slices, probe_wave, propagator_phase, intensity, centres, batch_order):
    slices = object_slices.shape[0]
    half = object_slices.shape[2]
    width = probe_wave.shape[1]
    size = half + width
    slot_count = centres.shape[2]
    rows, cols = lax.axis_size("row"), lax.axis_size("col")
    block_rows, block_cols = width // rows, width // cols
    lanes = max(block_cols, 128)
    row_bits, col_bits = rows.bit_length() - 1, cols.bit_length() - 1
    smem = pl.BlockSpec(memory_space=pltpu.SMEM)
    vmem = pl.BlockSpec(memory_space=pltpu.VMEM)

    def floats(*shape):
        return pltpu.VMEM(shape, jnp.float32)

    def sems(count):
        return pltpu.SemaphoreType.DMA((count,))

    slot_fields = floats(2, slot_count * width, width)
    constants, twiddles = tables(width)
    scratch = [
        pltpu.VMEM(probe_wave.shape, probe_wave.dtype),
        pltpu.VMEM(propagator_phase.shape, propagator_phase.dtype),
        pltpu.VMEM(intensity.shape[2:], intensity.dtype),
        pltpu.VMEM(constants.shape, jnp.bfloat16),
        floats(*twiddles.shape),
        [[floats(size, size)] * 2] * slices,
        [[floats(size, size)] * 2] * slices,
        slot_fields,
        slot_fields,
        slot_fields,
        floats(2, width, width),
        floats(slot_count * width, width),
        [[floats(size, half)] * 2] * slices,
        [[floats(half, size)] * 2] * slices,
        [[[floats(half, half)] * 2] * 2] * slices,
        [floats(size, half)] * slices,
        [floats(half, size)] * slices,
        [floats(2, rows >> (k + 1), 2, block_rows, width) for k in range(row_bits)],
        [floats(2, rows >> (k + 1), block_rows, width) for k in range(row_bits)],
        [floats(2, cols >> (k + 1), 2, block_rows, lanes) for k in range(col_bits)],
        [floats(2, cols >> (k + 1), block_rows, lanes) for k in range(col_bits)],
        sems(5 + 2 * slices),
        sems(8 * slices),
        sems(8 * slices),
        sems(8 * slices),
        sems(8 * slices),
        sems(row_bits + col_bits),
        sems(row_bits + col_bits),
    ]
    flops = slot_count * 6 * 2 * 3 * 2 * width * 2 * width * width
    return pl.pallas_call(
        kernel,
        out_shape=(
            jax.ShapeDtypeStruct(object_slices.shape, jnp.float32),
            jax.ShapeDtypeStruct((2, block_rows, block_cols), jnp.float32),
        ),
        in_specs=[smem] * 2 + [pl.BlockSpec(memory_space=pl.ANY)] * 6,
        out_specs=(vmem, vmem),
        scratch_shapes=scratch,
        compiler_params=pltpu.CompilerParams(
            vmem_limit_bytes=60 * 2**20, collective_id=0, has_side_effects=True
        ),
        cost_estimate=pl.CostEstimate(flops=flops, bytes_accessed=8 * 2**20, transcendentals=0),
    )(
        centres[0, 0], batch_order[0, 0], object_slices, probe_wave, propagator_phase,
        intensity[0, 0], jnp.asarray(constants), jnp.asarray(twiddles),
    )


def solution(mesh):
    placed = (
        P(None, None, "row", "col"),
        P(),
        P(),
        P("row", "col", None, None, None),
        P("row", "col", None, None),
        P("row", "col", None),
    )
    return jax.shard_map(
        per_device,
        mesh=mesh,
        in_specs=placed,
        out_specs=(P(None, None, "row", "col"), P(None, "row", "col")),
        check_vma=False,
    )
```
